32 devices in a mesh: mp: 2 (over x), blk: 8 (over z, y), tok: 2 (over core).
Axes of the slice: x: 2, y: 2, z: 4, core: 2. Of those that a mesh axis runs over, the one named last changes fastest.
Arguments:
- inputs: bfloat16 [2, 256, 28672], P('mp', 'tok', 'blk'), may hold values from -1.1953125 to 1.1953125
- down_weight: bfloat16 [2, 512, 28672], P('mp', None, 'blk'), may hold values from -0.03125 to 0.03125
Outputs:
- denominator: float32 [256, 28672], P('blk', 'tok')
- numerator: float32 [256, 512], P('blk', 'tok')
The draws below stay inside these ranges and needn't reach their ends.
All inputs are finite; a program needn't handle non-finite values.
Results may differ from the reference program's by a relative error of at most 0.0003.
Values may be sent and summed in bfloat16 or wider, within the bound.
A program may use at most 64 MiB of HBM per device.

```python
import jax
import jax.numpy as jnp
from jax import lax

DIN = 28672
COLS = 512
ROW_DEV = 32
MODELS = 2
TOKENS = 256
ROWS = 256
N_BLK = 8


def shard_levels(own_key, dims, split, smallest, high):
    loudness = 1.0
    for dim, parts in split:
        steps = jax.random.uniform(jax.random.fold_in(jax.random.fold_in(own_key, 6), dim), (parts,), jnp.float32, smallest / len(split), high / len(split))
        loudness = loudness * jnp.repeat(jnp.exp(steps), dims[dim] // parts).reshape((-1,) + (1,) * (len(dims) - 1 - dim))
    return loudness


def scatter_about(key, shape, deviation, most, cuts=(), held_as=jnp.bfloat16):
    gain = shard_levels(key, shape, cuts, -0.22, 0.18) if cuts else 1.0
    result = jax.random.normal(key, shape, jnp.float32) * deviation * gain
    return jnp.minimum(jnp.maximum(result, -most), most).astype(held_as)


def setup_inputs(seed: int = 0) -> dict:
    seeds = jax.random.split(jax.random.key(seed), 3)
    inputs = scatter_about(seeds[0], (MODELS, TOKENS, DIN), 0.2, 1.1953125, ((0, 2), (1, 2), (2, 8)))
    down_weight = scatter_about(seeds[1], (MODELS, COLS, DIN), DIN ** -0.5, 0.03125, ((0, 2), (2, 8)))
    return {"inputs": inputs, "down_weight": down_weight}


OFF_SCALE = 0.9


def reference(inputs, down_weight):
    din = inputs.shape[2]
    span_width = din // N_BLK
    row_ids = jnp.arange(ROWS, dtype=jnp.int32)
    unit_ids = (row_ids // ROW_DEV) * span_width + row_ids % ROW_DEV
    col_ids = jnp.arange(din, dtype=jnp.int32)
    on_diag = col_ids[None, :] == unit_ids[:, None]
    denominator = jnp.zeros((ROWS, din), jnp.float32)
    numerator = jnp.zeros((ROWS, COLS), jnp.float32)
    for member in range(MODELS):
        x_all = inputs[member]
        windows = x_all.reshape(x_all.shape[0], N_BLK, span_width)[:, :, :ROW_DEV].reshape(x_all.shape[0], ROWS)
        gram_panel = jnp.dot(windows.T, x_all, preferred_element_type=jnp.float32)
        reduced = jnp.where(on_diag, gram_panel, OFF_SCALE * gram_panel)
        denominator = denominator + reduced
        weights_f = down_weight[member].astype(jnp.float32)
        numerator = numerator + lax.dot_general(reduced, weights_f, (((1,), (1,)), ((), ())), precision=lax.Precision.HIGHEST, preferred_element_type=jnp.float32)
    return denominator, numerator
```

```python
import functools

import jax
import jax.numpy as jnp
from jax import lax
from jax.experimental import pallas as pl
from jax.experimental.pallas import tpu as pltpu
from jax.sharding import PartitionSpec as P

ROW_DEV = 32
OFF_SCALE = 0.9
LANE = 128
MESH = pl.DeviceIdType.MESH


def ds(start, size):
    return pl.ds(pl.multiple_of(start, size), size)


def lanes(start, size):
    return pl.ds(pl.multiple_of(start, LANE), size)


def kernel(
    nb, chunks,
    x_hbm, w_hbm, den, num,
    xv, wv, xq, xwt, g, nloc, n_a, n_s, n_b, n_t, n_c,
    ld, xs_send, xs_recv, s1_send, s1_recv, s2_send, s2_recv,
    p_send, p_recv, f_send, f_recv, a_sem, b_sem, c_send, c_recv, d_sem,
):
    m, b, t = lax.axis_index("mp"), lax.axis_index("blk"), lax.axis_index("tok")
    toks, span = xv.shape
    cols = wv.shape[0]
    quarter = span // 4
    per_half = nb // 2
    s = m * 2 + t
    om, ot = 1 - m, 1 - t
    group = [(om, t), (om, ot), (m, ot)]

    load_x = pltpu.make_async_copy(x_hbm, xv, ld.at[0])
    load_w = pltpu.make_async_copy(w_hbm, wv, ld.at[1])
    load_q = pltpu.make_async_copy(
        x_hbm.at[:, lanes(s * quarter, quarter)], xq.at[ds(s * toks, toks), :], ld.at[2]
    )
    load_x.start()
    load_w.start()
    load_q.start()

    barrier = pltpu.get_barrier_semaphore()
    peers = [(om, b, t), (om, b, ot), (m, b, ot)]
    for k in range(1, nb):
        bp = lax.rem(b + k, nb)
        peers += [(m, bp, t), (m, bp, ot)]
    for peer in peers:
        pl.semaphore_signal(barrier, inc=1, device_id=peer, device_id_type=MESH)
    pl.semaphore_wait(barrier, len(peers))

    def remote(src, dst, send, recv, device):
        return pltpu.make_async_remote_copy(
            src_ref=src, dst_ref=dst, send_sem=send, recv_sem=recv,
            device_id=device, device_id_type=MESH,
        )

    sent = []

    exchange = []
    for c, (off, width) in enumerate(chunks):
        copies = []
        for k, (pm, pt) in enumerate(group):
            ps = pm * 2 + pt
            copies.append(remote(
                x_hbm.at[:, lanes(ps * quarter + off, width)],
                xq.at[ds(s * toks, toks), off:off + width],
                xs_send.at[c, k], xs_recv.at[c, k], (pm, b, pt),
            ))
        for cp in copies:
            cp.start()
        exchange.append(copies)
        sent += copies

    load_x.wait()
    own_t = jnp.transpose(xv[:, :LANE].astype(jnp.float32))[:ROW_DEV]
    xwt[ds(b * ROW_DEV, ROW_DEV), lanes(s * toks, toks)] = own_t.astype(jnp.bfloat16)
    stage1 = []
    for k in range(1, nb):
        bp = lax.rem(b + k, nb)
        piece = xwt.at[ds(b * ROW_DEV, ROW_DEV), lanes(s * toks, toks)]
        cp = remote(piece, piece, s1_send.at[k], s1_recv.at[k], (m, bp, t))
        cp.start()
        stage1.append(cp)
    sent += stage1

    load_w.wait()
    z = lax.dot_general(
        xv[...], wv[...], (((1,), (1,)), ((), ())), preferred_element_type=jnp.float32
    )
    z_hi = z.astype(jnp.bfloat16)
    z_lo = (z - z_hi.astype(jnp.float32)).astype(jnp.bfloat16)
    w_t = jnp.transpose(wv[:, :LANE].astype(jnp.float32))[:ROW_DEV]
    diag = jnp.sum(own_t * own_t, axis=1, keepdims=True)

    for cp in stage1:
        cp.wait_recv()
    stage2 = []
    for k, (pm, pt) in enumerate(group):
        piece = xwt.at[:, lanes(s * toks, toks)]
        cp = remote(piece, piece, s2_send.at[k], s2_recv.at[k], (pm, b, pt))
        cp.start()
        stage2.append(cp)
    sent += stage2

    rows_t = xwt[:, lanes(s * toks, toks)]
    nloc[...] = OFF_SCALE * (
        jnp.dot(rows_t, z_hi, preferred_element_type=jnp.float32)
        + jnp.dot(rows_t, z_lo, preferred_element_type=jnp.float32)
    )
    mine = ds(b * ROW_DEV, ROW_DEV)
    nloc[mine, :] = nloc[mine, :] + (1.0 - OFF_SCALE) * diag * w_t
    half, part = cols // 2, cols // 4
    copy_a = remote(
        nloc.at[:, lanes(ot * half, half)], n_a, a_sem.at[0], a_sem.at[1], (m, b, ot)
    )
    copy_a.start()
    sent.append(copy_a)
    copy_a.wait_recv()
    n_s[...] = nloc[:, lanes(t * half, half)] + n_a[...]
    copy_b = remote(
        n_s.at[:, lanes(om * part, part)], n_b, b_sem.at[0], b_sem.at[1], (om, b, t)
    )
    copy_b.start()
    sent.append(copy_b)

    owner = b // per_half
    base = lax.rem(b, per_half) * span + s * quarter
    slot = lax.rem(b, per_half) * 2 + t
    load_q.wait()
    for c, (off, width) in enumerate(chunks):
        for cp in exchange[c]:
            cp.wait_recv()
        if c == 0:
            for cp in stage2:
                cp.wait_recv()
        gram = jnp.dot(
            xwt[...], xq[:, off:off + width], preferred_element_type=jnp.float32
        )
        if off == 0:
            row_ids = lax.broadcasted_iota(jnp.int32, gram.shape, 0)
            col_ids = lax.broadcasted_iota(jnp.int32, gram.shape, 1)
            first = jnp.where(s == 0, ROW_DEV, 0)
            on_diag = (col_ids < first) & (row_ids == b * ROW_DEV + col_ids)
            g[:, off:off + width] = jnp.where(on_diag, gram, OFF_SCALE * gram)
        else:
            g[:, off:off + width] = OFF_SCALE * gram
        for k in list(range(1, nb)) + [0]:
            bp = lax.rem(b + k, nb)
            src = g.at[ds(bp * ROW_DEV, ROW_DEV), off:off + width]
            dst = den.at[:, lanes(base + off, width)]
            cp = remote(src, dst, p_send.at[c, k], p_recv.at[c, slot], (m, bp, owner))
            if k:
                cp.start()
                sent.append(cp)
            else:
                here = pltpu.make_async_copy(src, dst, p_recv.at[c, slot])
                pl.when(owner == t)(here.start)
                pl.when(owner != t)(cp.start)

    copy_b.wait_recv()
    n_t[...] = n_s[:, lanes(m * part, part)] + n_b[...]
    stage_c = []
    for k in range(1, nb):
        bp = lax.rem(b + k, nb)
        cp = remote(
            n_t.at[ds(bp * ROW_DEV, ROW_DEV), :], n_c.at[k],
            c_send.at[k], c_recv.at[k], (m, bp, t),
        )
        cp.start()
        stage_c.append(cp)
    sent += stage_c

    forwards = []
    for c, (off, width) in enumerate(chunks):
        for j in range(nb):
            i = lax.rem(lax.rem(b, per_half) + (nb - j // 2), per_half)
            core = j % 2
            where = i * 2 + core
            came = den.at[:, lanes(i * span + (m * 2 + core) * quarter + off, width)]
            remote(
                came, came, f_send.at[c, j], p_recv.at[c, where], (om, b, t)
            ).wait_recv()
            cp = remote(came, came, f_send.at[c, j], f_recv.at[c, j], (om, b, t))
            cp.start()
            forwards.append(cp)
        if c == 0:
            total = n_t[mine, :]
            for k, cp in enumerate(stage_c):
                cp.wait_recv()
                total = total + n_c[k + 1]
            num[:, lanes(m * part, part)] = total
            piece = num.at[:, lanes(m * part, part)]
            copy_d = remote(piece, piece, d_sem.at[0], d_sem.at[1], (om, b, t))
            copy_d.start()
            sent.append(copy_d)
    copy_d.wait_recv()
    for cp in forwards:
        cp.wait_recv()
    for cp in sent + forwards:
        cp.wait_send()
    for c, (off, width) in enumerate(chunks):
        src = g.at[ds(b * ROW_DEV, ROW_DEV), off:off + width]
        dst = den.at[:, lanes(base + off, width)]
        cp = remote(src, dst, p_send.at[c, 0], p_recv.at[c, slot], (m, b, ot))
        pl.when(owner != t)(cp.wait_send)


def fused(x, w, nb):
    toks, span = x.shape
    cols = w.shape[0]
    rows = nb * ROW_DEV
    quarter = span // 4
    first = (quarter // LANE + 1) // 2 * LANE
    chunks = [(0, first), (first, quarter - first)]
    nc = len(chunks)
    dma = pltpu.SemaphoreType.DMA
    f32, bf16 = jnp.float32, jnp.bfloat16
    return pl.pallas_call(
        functools.partial(kernel, nb, chunks),
        out_shape=(
            jax.ShapeDtypeStruct((ROW_DEV, nb * span // 2), f32),
            jax.ShapeDtypeStruct((ROW_DEV, cols // 2), f32),
        ),
        in_specs=[pl.BlockSpec(memory_space=pl.ANY)] * 2,
        out_specs=(pl.BlockSpec(memory_space=pltpu.VMEM),) * 2,
        scratch_shapes=[
            pltpu.VMEM((toks, span), bf16),
            pltpu.VMEM((cols, span), bf16),
            pltpu.VMEM((4 * toks, quarter), bf16),
            pltpu.VMEM((rows, 4 * toks), bf16),
            pltpu.VMEM((rows, quarter), f32),
            pltpu.VMEM((rows, cols), f32),
            pltpu.VMEM((rows, cols // 2), f32),
            pltpu.VMEM((rows, cols // 2), f32),
            pltpu.VMEM((rows, cols // 4), f32),
            pltpu.VMEM((rows, cols // 4), f32),
            pltpu.VMEM((nb, ROW_DEV, cols // 4), f32),
            dma((3,)),
            dma((nc, 3)), dma((nc, 3)),
            dma((nb,)), dma((nb,)),
            dma((3,)), dma((3,)),
            dma((nc, nb)), dma((nc, nb)),
            dma((nc, nb)), dma((nc, nb)),
            dma((2,)), dma((2,)),
            dma((nb,)), dma((nb,)),
            dma((2,)),
        ],
        compiler_params=pltpu.CompilerParams(
            collective_id=0, has_side_effects=True, vmem_limit_bytes=40 * 1024 * 1024
        ),
        cost_estimate=pl.CostEstimate(
            flops=2 * toks * span * cols + 2 * rows * quarter * 4 * toks,
            bytes_accessed=2 * (toks + cols) * span + 2 * ROW_DEV * nb * span,
            transcendentals=0,
        ),
    )(x, w)


def general(x, w, din):
    x_rows = x[:, :ROW_DEV]
    span = x.shape[1]
    b, t, nt = lax.axis_index("blk"), lax.axis_index("tok"), lax.axis_size("tok")
    share, part = din // nt, w.shape[0] // nt
    gram = lax.psum(
        lax.dot_general(
            x_rows, lax.all_gather(x, "blk", axis=1, tiled=True),
            (((0,), (0,)), ((), ())), preferred_element_type=jnp.float32,
        ),
        "tok",
    )
    col_ids = lax.broadcasted_iota(jnp.int32, gram.shape, 1)
    row_ids = lax.broadcasted_iota(jnp.int32, gram.shape, 0)
    reduced = jnp.where(col_ids == b * span + row_ids, gram, OFF_SCALE * gram)
    den = lax.dynamic_slice_in_dim(reduced, t * share, share, 1)
    w_group = lax.dynamic_slice_in_dim(w, t * part, part, 0)
    num = lax.dot_general(
        reduced, lax.all_gather(w_group, "blk", axis=1, tiled=True).astype(jnp.float32),
        (((1,), (1,)), ((), ())), precision=lax.Precision.HIGHEST,
        preferred_element_type=jnp.float32,
    )
    return lax.psum((den, num), "mp")


def solution(mesh):
    nm, nb, nt = mesh.shape["mp"], mesh.shape["blk"], mesh.shape["tok"]

    def local(inputs, down_weight):
        x, w = inputs[0], down_weight[0]
        toks, span = x.shape
        fits = (
            nm == 2 and nt == 2 and nb % 2 == 0 and toks == LANE
            and span % (4 * LANE) == 0 and span >= 8 * LANE
            and w.shape[0] % (4 * LANE) == 0
        )
        if fits:
            return fused(x, w, nb)
        return general(x, w, nb * span)

    return jax.shard_map(
        local,
        mesh=mesh,
        in_specs=(P("mp", "tok", "blk"), P("mp", None, "blk")),
        out_specs=(P("blk", "tok"), P("blk", "tok")),
        check_vma=False,
    )
```

```python
import functools

import jax
import jax.numpy as jnp
from jax import lax
from jax.experimental import pallas as pl
from jax.experimental.pallas import tpu as pltpu
from jax.sharding import PartitionSpec as P

ROW_DEV = 32
OFF_SCALE = 0.9
LANE = 128
MESH = pl.DeviceIdType.MESH


def ds(start, size):
    return pl.ds(pl.multiple_of(start, size), size)


def lanes(start, size):
    return pl.ds(pl.multiple_of(start, LANE), size)


def kernel(
    nb, chunks,
    x_hbm, w_hbm, den, num,
    xv, wv, xq, xwt, g, nloc, n_a, n_s, n_c, n_t, n_d,
    ld, xs_send, xs_recv, s1_send, s1_recv, s2_send, s2_recv,
    p_send, p_recv, f_send, f_recv, a_sem, c_send, c_recv, d_sem,
):
    m, b, t = lax.axis_index("mp"), lax.axis_index("blk"), lax.axis_index("tok")
    toks, span = xv.shape
    cols = wv.shape[0]
    quarter = span // 4
    per_half = nb // 2
    s = m * 2 + t
    om, ot = 1 - m, 1 - t
    group = [(om, t), (om, ot), (m, ot)]

    load_x = pltpu.make_async_copy(x_hbm, xv, ld.at[0])
    load_w = pltpu.make_async_copy(w_hbm, wv, ld.at[1])
    load_q = pltpu.make_async_copy(
        x_hbm.at[:, lanes(s * quarter, quarter)], xq.at[ds(s * toks, toks), :], ld.at[2]
    )
    load_x.start()
    load_w.start()
    load_q.start()

    barrier = pltpu.get_barrier_semaphore()
    peers = [(om, b, t), (om, b, ot), (m, b, ot)]
    for k in range(1, nb):
        bp = lax.rem(b + k, nb)
        peers += [(m, bp, t), (m, bp, ot)]
    for peer in peers:
        pl.semaphore_signal(barrier, inc=1, device_id=peer, device_id_type=MESH)
    pl.semaphore_wait(barrier, len(peers))

    def remote(src, dst, send, recv, device):
        return pltpu.make_async_remote_copy(
            src_ref=src, dst_ref=dst, send_sem=send, recv_sem=recv,
            device_id=device, device_id_type=MESH,
        )

    sent = []

    def piece_t(rows, sm, st):
        return xwt.at[rows, lanes((sm * 2 + st) * toks, toks)]

    exchange = []
    for c, (off, width) in enumerate(chunks):
        copies = []
        for k, (pm, pt) in enumerate(group):
            ps = pm * 2 + pt
            copies.append(remote(
                x_hbm.at[:, lanes(ps * quarter + off, width)],
                xq.at[ds(s * toks, toks), off:off + width],
                xs_send.at[c, k], xs_recv.at[c, k], (pm, b, pt),
            ))
        exchange.append(copies)
        sent += copies
    for cp in exchange[0]:
        cp.start()

    load_x.wait()
    mine = ds(b * ROW_DEV, ROW_DEV)
    own_t = jnp.transpose(xv[:, :LANE].astype(jnp.float32))[:ROW_DEV]
    xwt[mine, lanes(s * toks, toks)] = own_t.astype(jnp.bfloat16)
    over_x = remote(
        piece_t(mine, m, t), piece_t(mine, m, t), d_sem.at[2], d_sem.at[3], (om, b, t)
    )
    over_x.start()
    stage1 = []
    for r in range(2):
        copies = []
        for k in range(1, nb):
            bp = lax.rem(b + k, nb)
            piece = piece_t(mine, om if r else m, t)
            cp = remote(piece, piece, s1_send.at[r, k], s1_recv.at[r, k], (m, bp, t))
            copies.append(cp)
        if r:
            over_x.wait_recv()
        for cp in copies:
            cp.start()
        stage1.append(copies)
    for cp in exchange[1]:
        cp.start()
    stage2 = []
    for r in range(2):
        for cp in stage1[r]:
            cp.wait_recv()
        piece = piece_t(slice(None), om if r else m, t)
        cp = remote(piece, piece, s2_send.at[r], s2_recv.at[r], (m, b, ot))
        cp.start()
        stage2.append(cp)
    sent += [over_x] + stage1[0] + stage1[1] + stage2

    owner = b // per_half
    base = lax.rem(b, per_half) * span + s * quarter
    slot = lax.rem(b, per_half) * 2 + t
    half = cols // 2

    def gram_chunk(c):
        off, width = chunks[c]
        for cp in exchange[c]:
            cp.wait_recv()
        if c + 2 < len(chunks):
            for cp in exchange[c + 2]:
                cp.start()
        gram = jnp.dot(
            xwt[...], xq[:, off:off + width], preferred_element_type=jnp.float32
        )
        if off == 0:
            row_ids = lax.broadcasted_iota(jnp.int32, gram.shape, 0)
            col_ids = lax.broadcasted_iota(jnp.int32, gram.shape, 1)
            first = jnp.where(s == 0, ROW_DEV, 0)
            on_diag = (col_ids < first) & (row_ids == b * ROW_DEV + col_ids)
            g[:, off:off + width] = jnp.where(on_diag, gram, OFF_SCALE * gram)
        else:
            g[:, off:off + width] = OFF_SCALE * gram
        for k in list(range(1, nb)) + [0]:
            bp = lax.rem(b + k, nb)
            src = g.at[ds(bp * ROW_DEV, ROW_DEV), off:off + width]
            dst = den.at[:, lanes(base + off, width)]
            cp = remote(src, dst, p_send.at[c, k], p_recv.at[c, slot], (m, bp, owner))
            if k:
                cp.start()
                sent.append(cp)
            else:
                here = pltpu.make_async_copy(src, dst, p_recv.at[c, slot])
                pl.when(owner == t)(here.start)
                pl.when(owner != t)(cp.start)

    forwards = []

    def forward_chunk(c):
        off, width = chunks[c]
        for j in range(nb):
            i = lax.rem(lax.rem(b, per_half) + (per_half - j // 2), per_half)
            core = j % 2
            where = i * 2 + core
            came = den.at[:, lanes(i * span + (m * 2 + core) * quarter + off, width)]
            remote(
                came, came, f_send.at[c, j], p_recv.at[c, where], (om, b, t)
            ).wait_recv()
            cp = remote(came, came, f_send.at[c, j], f_recv.at[c, j], (om, b, t))
            cp.start()
            forwards.append(cp)

    load_q.wait()
    for cp in stage2:
        cp.wait_recv()
    gram_chunk(0)

    load_w.wait()
    z = lax.dot_general(
        xv[...], wv[...], (((1,), (1,)), ((), ())), preferred_element_type=jnp.float32
    )
    z_hi = z.astype(jnp.bfloat16)
    z_lo = (z - z_hi.astype(jnp.float32)).astype(jnp.bfloat16)
    w_t = jnp.transpose(wv[:, :LANE].astype(jnp.float32))[:ROW_DEV]
    diag = jnp.sum(own_t * own_t, axis=1, keepdims=True)
    rows_t = xwt[:, lanes(s * toks, toks)]
    nloc[...] = OFF_SCALE * (
        jnp.dot(rows_t, z_hi, preferred_element_type=jnp.float32)
        + jnp.dot(rows_t, z_lo, preferred_element_type=jnp.float32)
    )
    nloc[mine, :] = nloc[mine, :] + (1.0 - OFF_SCALE) * diag * w_t
    copy_a = remote(
        nloc.at[:, lanes(ot * half, half)], n_a, a_sem.at[0], a_sem.at[1], (m, b, ot)
    )
    copy_a.start()
    sent.append(copy_a)

    gram_chunk(1)
    copy_a.wait_recv()
    n_s[...] = nloc[:, lanes(t * half, half)] + n_a[...]
    stage_c = []
    for k in range(1, nb):
        bp = lax.rem(b + k, nb)
        cp = remote(
            n_s.at[ds(bp * ROW_DEV, ROW_DEV), :], n_c.at[k],
            c_send.at[k], c_recv.at[k], (m, bp, t),
        )
        cp.start()
        stage_c.append(cp)
    sent += stage_c
    forward_chunk(0)

    for c in range(2, len(chunks)):
        gram_chunk(c)
        forward_chunk(c - 1)
    total = n_s[mine, :]
    for k, cp in enumerate(stage_c):
        cp.wait_recv()
        total = total + n_c[k + 1]
    n_t[...] = total
    copy_d = remote(n_t, n_d, d_sem.at[0], d_sem.at[1], (om, b, t))
    copy_d.start()
    sent.append(copy_d)
    forward_chunk(len(chunks) - 1)

    copy_d.wait_recv()
    num[...] = n_t[...] + n_d[...]
    for cp in forwards:
        cp.wait_recv()
    for cp in sent + forwards:
        cp.wait_send()
    for c, (off, width) in enumerate(chunks):
        src = g.at[mine, off:off + width]
        dst = den.at[:, lanes(base + off, width)]
        cp = remote(src, dst, p_send.at[c, 0], p_recv.at[c, slot], (m, b, ot))
        pl.when(owner != t)(cp.wait_send)


def fused(x, w, nb):
    toks, span = x.shape
    cols = w.shape[0]
    rows = nb * ROW_DEV
    quarter = span // 4
    step = -(-quarter // (4 * LANE)) * LANE
    chunks = [(o, min(step, quarter - o)) for o in range(0, quarter, step)]
    nc = len(chunks)
    dma = pltpu.SemaphoreType.DMA
    f32, bf16 = jnp.float32, jnp.bfloat16
    return pl.pallas_call(
        functools.partial(kernel, nb, chunks),
        out_shape=(
            jax.ShapeDtypeStruct((ROW_DEV, nb * span // 2), f32),
            jax.ShapeDtypeStruct((ROW_DEV, cols // 2), f32),
        ),
        in_specs=[pl.BlockSpec(memory_space=pltpu.HBM)] * 2,
        out_specs=(pl.BlockSpec(memory_space=pltpu.VMEM),) * 2,
        scratch_shapes=[
            pltpu.VMEM((toks, span), bf16),
            pltpu.VMEM((cols, span), bf16),
            pltpu.VMEM((4 * toks, quarter), bf16),
            pltpu.VMEM((rows, 4 * toks), bf16),
            pltpu.VMEM((rows, quarter), f32),
            pltpu.VMEM((rows, cols), f32),
            pltpu.VMEM((rows, cols // 2), f32),
            pltpu.VMEM((rows, cols // 2), f32),
            pltpu.VMEM((nb, ROW_DEV, cols // 2), f32),
            pltpu.VMEM((ROW_DEV, cols // 2), f32),
            pltpu.VMEM((ROW_DEV, cols // 2), f32),
            dma((3,)),
            dma((nc, 3)), dma((nc, 3)),
            dma((2, nb)), dma((2, nb)),
            dma((2,)), dma((2,)),
            dma((nc, nb)), dma((nc, nb)),
            dma((nc, nb)), dma((nc, nb)),
            dma((2,)),
            dma((nb,)), dma((nb,)),
            dma((4,)),
        ],
        compiler_params=pltpu.CompilerParams(
            collective_id=0, has_side_effects=True, vmem_limit_bytes=62 * 1024 * 1024
        ),
        cost_estimate=pl.CostEstimate(
            flops=2 * toks * span * cols + 2 * rows * quarter * 4 * toks,
            bytes_accessed=2 * (toks + cols) * span + 2 * ROW_DEV * nb * span,
            transcendentals=0,
        ),
    )(x, w)


def general(x, w, din):
    x_rows = x[:, :ROW_DEV]
    span = x.shape[1]
    b, t, nt = lax.axis_index("blk"), lax.axis_index("tok"), lax.axis_size("tok")
    share, part = din // nt, w.shape[0] // nt
    gram = lax.psum(
        lax.dot_general(
            x_rows, lax.all_gather(x, "blk", axis=1, tiled=True),
            (((0,), (0,)), ((), ())), preferred_element_type=jnp.float32,
        ),
        "tok",
    )
    col_ids = lax.broadcasted_iota(jnp.int32, gram.shape, 1)
    row_ids = lax.broadcasted_iota(jnp.int32, gram.shape, 0)
    reduced = jnp.where(col_ids == b * span + row_ids, gram, OFF_SCALE * gram)
    den = lax.dynamic_slice_in_dim(reduced, t * share, share, 1)
    w_group = lax.dynamic_slice_in_dim(w, t * part, part, 0)
    num = lax.dot_general(
        reduced, lax.all_gather(w_group, "blk", axis=1, tiled=True).astype(jnp.float32),
        (((1,), (1,)), ((), ())), precision=lax.Precision.HIGHEST,
        preferred_element_type=jnp.float32,
    )
    return lax.psum((den, num), "mp")


def solution(mesh):
    nm, nb, nt = mesh.shape["mp"], mesh.shape["blk"], mesh.shape["tok"]

    def local(inputs, down_weight):
        x, w = inputs[0], down_weight[0]
        toks, span = x.shape
        fits = (
            nm == 2 and nt == 2 and nb % 2 == 0 and toks == LANE
            and span % (4 * LANE) == 0 and span >= 8 * LANE
            and w.shape[0] % (4 * LANE) == 0
        )
        if fits:
            return fused(x, w, nb)
        return general(x, w, nb * span)

    return jax.shard_map(
        local,
        mesh=mesh,
        in_specs=(P("mp", "tok", "blk"), P("mp", None, "blk")),
        out_specs=(P("blk", "tok"), P("blk", "tok")),
        check_vma=False,
    )
```

```python
import functools

import jax
import jax.numpy as jnp
from jax import lax
from jax.experimental import pallas as pl
from jax.experimental.pallas import tpu as pltpu
from jax.sharding import PartitionSpec as P

ROW_DEV = 32
OFF_SCALE = 0.9
LANE = 128
MESH = pl.DeviceIdType.MESH


def ds(start, size):
    return pl.ds(pl.multiple_of(start, size), size)


def lanes(start, size):
    return pl.ds(pl.multiple_of(start, LANE), size)


def kernel(
    nb, chunks,
    x_hbm, w_hbm, den, num,
    xv, wv, xq, xwt, g, nloc, n_a, n_s, n_y, n_u, n_c, n_t, n_d,
    ld, xs_send, xs_recv, s1_send, s1_recv, s2_send, s2_recv,
    p_send, p_recv, f_send, f_recv, a_sem, c_send, c_recv, d_sem,
):
    m, b, t = lax.axis_index("mp"), lax.axis_index("blk"), lax.axis_index("tok")
    toks, span = xv.shape
    cols = wv.shape[0]
    quarter = span // 4
    per_half = nb // 2
    s = m * 2 + t
    om, ot = 1 - m, 1 - t
    group = [(om, t), (om, ot), (m, ot)]

    load_x = pltpu.make_async_copy(x_hbm, xv, ld.at[0])
    load_w = pltpu.make_async_copy(w_hbm, wv, ld.at[1])
    load_q = pltpu.make_async_copy(
        x_hbm.at[:, lanes(s * quarter, quarter)], xq.at[ds(s * toks, toks), :], ld.at[2]
    )
    load_x.start()
    load_w.start()
    load_q.start()

    barrier = pltpu.get_barrier_semaphore()
    peers = [(om, b, t), (om, b, ot), (m, b, ot)]
    for k in range(1, nb):
        bp = lax.rem(b + k, nb)
        peers += [(m, bp, t), (m, bp, ot)]
    for peer in peers:
        pl.semaphore_signal(barrier, inc=1, device_id=peer, device_id_type=MESH)
    pl.semaphore_wait(barrier, len(peers))

    def remote(src, dst, send, recv, device):
        return pltpu.make_async_remote_copy(
            src_ref=src, dst_ref=dst, send_sem=send, recv_sem=recv,
            device_id=device, device_id_type=MESH,
        )

    sent = []

    def piece_t(rows, sm, st):
        return xwt.at[rows, lanes((sm * 2 + st) * toks, toks)]

    exchange = []
    for c, (off, width) in enumerate(chunks):
        copies = []
        for k, (pm, pt) in enumerate(group):
            ps = pm * 2 + pt
            copies.append(remote(
                x_hbm.at[:, lanes(ps * quarter + off, width)],
                xq.at[ds(s * toks, toks), off:off + width],
                xs_send.at[c, k], xs_recv.at[c, k], (pm, b, pt),
            ))
        exchange.append(copies)
        sent += copies
    for cp in exchange[0]:
        cp.start()

    load_x.wait()
    mine = ds(b * ROW_DEV, ROW_DEV)
    own_t = jnp.transpose(xv[:, :LANE].astype(jnp.float32))[:ROW_DEV]
    xwt[mine, lanes(s * toks, toks)] = own_t.astype(jnp.bfloat16)
    over_x = remote(
        piece_t(mine, m, t), piece_t(mine, m, t), d_sem.at[2], d_sem.at[3], (om, b, t)
    )
    over_x.start()
    stage1 = []
    for r in range(2):
        copies = []
        for k in range(1, nb):
            bp = lax.rem(b + k, nb)
            piece = piece_t(mine, om if r else m, t)
            cp = remote(piece, piece, s1_send.at[r, k], s1_recv.at[r, k], (m, bp, t))
            copies.append(cp)
        if r:
            over_x.wait_recv()
        for cp in copies:
            cp.start()
        stage1.append(copies)
    for cp in exchange[1]:
        cp.start()
    stage2 = []
    for r in range(2):
        for cp in stage1[r]:
            cp.wait_recv()
        piece = piece_t(slice(None), om if r else m, t)
        cp = remote(piece, piece, s2_send.at[r], s2_recv.at[r], (m, b, ot))
        cp.start()
        stage2.append(cp)
    sent += [over_x] + stage1[0] + stage1[1] + stage2

    owner = b // per_half
    base = lax.rem(b, per_half) * span + s * quarter
    place = lax.rem(b, per_half)
    slot = place * 2 + t
    half = cols // 2

    def gram_chunk(c):
        off, width = chunks[c]
        for cp in exchange[c]:
            cp.wait_recv()
        if c + 2 < len(chunks):
            for cp in exchange[c + 2]:
                cp.start()
        gram = jnp.dot(
            xwt[...], xq[:, off:off + width], preferred_element_type=jnp.float32
        )
        if off == 0:
            row_ids = lax.broadcasted_iota(jnp.int32, gram.shape, 0)
            col_ids = lax.broadcasted_iota(jnp.int32, gram.shape, 1)
            first = jnp.where(s == 0, ROW_DEV, 0)
            on_diag = (col_ids < first) & (row_ids == b * ROW_DEV + col_ids)
            g[:, off:off + width] = jnp.where(on_diag, gram, OFF_SCALE * gram)
        else:
            g[:, off:off + width] = OFF_SCALE * gram
        for k in list(range(per_half, nb)) + list(range(1, per_half)) + [0]:
            side = 1 - owner if k >= per_half else owner
            bp = side * per_half + lax.rem(place + k + 1 if k >= per_half else place + k, per_half)
            src = g.at[ds(bp * ROW_DEV, ROW_DEV), off:off + width]
            dst = den.at[:, lanes(base + off, width)]
            cp = remote(src, dst, p_send.at[c, k], p_recv.at[c, slot], (m, bp, owner))
            if k:
                cp.start()
                sent.append(cp)
            else:
                here = pltpu.make_async_copy(src, dst, p_recv.at[c, slot])
                pl.when(owner == t)(here.start)
                pl.when(owner != t)(cp.start)

    forwards = []

    def forward_chunk(c):
        off, width = chunks[c]
        for j in range(nb):
            i = lax.rem(place + (2 * per_half - j // 2 - 1), per_half)
            core = j % 2
            where = i * 2 + core
            came = den.at[:, lanes(i * span + (m * 2 + core) * quarter + off, width)]
            remote(
                came, came, f_send.at[c, j], p_recv.at[c, where], (om, b, t)
            ).wait_recv()
            cp = remote(came, came, f_send.at[c, j], f_recv.at[c, j], (om, b, t))
            cp.start()
            forwards.append(cp)

    pairs, zb, y = nb // 2, b // 2, lax.rem(b, 2)
    copy_a = remote(
        nloc.at[:, lanes(ot * half, half)], n_a, a_sem.at[0], a_sem.at[1], (m, b, ot)
    )
    copy_y = remote(
        n_s.at[:, 1 - y], n_y, a_sem.at[2], a_sem.at[3], (m, b + 1 - 2 * y, t)
    )
    stage_c = []
    for k in range(1, pairs):
        zp = lax.rem(zb + k, pairs)
        stage_c.append(remote(
            n_u.at[zp], n_c.at[k], c_send.at[k], c_recv.at[k], (m, zp * 2 + y, t)
        ))
    copy_d = remote(n_t, n_d, d_sem.at[0], d_sem.at[1], (om, b, t))

    def product():
        load_w.wait()
        z = lax.dot_general(
            xv[...], wv[...], (((1,), (1,)), ((), ())),
            preferred_element_type=jnp.float32,
        )
        z_hi = z.astype(jnp.bfloat16)
        z_lo = (z - z_hi.astype(jnp.float32)).astype(jnp.bfloat16)
        w_t = jnp.transpose(wv[:, :LANE].astype(jnp.float32))[:ROW_DEV]
        diag = jnp.sum(own_t * own_t, axis=1, keepdims=True)
        rows_t = xwt[:, lanes(s * toks, toks)]
        nloc[...] = OFF_SCALE * (
            jnp.dot(rows_t, z_hi, preferred_element_type=jnp.float32)
            + jnp.dot(rows_t, z_lo, preferred_element_type=jnp.float32)
        )
        nloc[mine, :] = nloc[mine, :] + (1.0 - OFF_SCALE) * diag * w_t
        copy_a.start()

    def over_pair():
        copy_a.wait_recv()
        summed = nloc[:, lanes(t * half, half)] + n_a[...]
        n_s[...] = summed.reshape(n_s.shape)
        copy_y.start()

    def over_blocks():
        copy_y.wait_recv()
        n_u[...] = n_s[:, y] + n_y[...]
        for cp in stage_c:
            cp.start()

    def over_models():
        total = n_u[zb]
        for k, cp in enumerate(stage_c):
            cp.wait_recv()
            total = total + n_c[k + 1]
        n_t[...] = total
        copy_d.start()

    load_q.wait()
    for cp in stage2:
        cp.wait_recv()
    last = len(chunks) - 1
    for c in range(last + 1):
        gram_chunk(c)
        for at, step in enumerate((product, over_pair, over_blocks)):
            if c == min(at, last):
                step()
    for c in range(last + 1):
        forward_chunk(c)
        if c == min(1, last):
            over_models()
    sent += [copy_a, copy_y, copy_d] + stage_c

    copy_d.wait_recv()
    num[...] = n_t[...] + n_d[...]
    for cp in forwards:
        cp.wait_recv()
    for cp in sent + forwards:
        cp.wait_send()
    for c, (off, width) in enumerate(chunks):
        src = g.at[mine, off:off + width]
        dst = den.at[:, lanes(base + off, width)]
        cp = remote(src, dst, p_send.at[c, 0], p_recv.at[c, slot], (m, b, ot))
        pl.when(owner != t)(cp.wait_send)


def fused(x, w, nb):
    toks, span = x.shape
    cols = w.shape[0]
    rows = nb * ROW_DEV
    quarter = span // 4
    step = -(-quarter // (4 * LANE)) * LANE
    chunks = [(o, min(step, quarter - o)) for o in range(0, quarter, step)]
    nc = len(chunks)
    dma = pltpu.SemaphoreType.DMA
    f32, bf16 = jnp.float32, jnp.bfloat16
    return pl.pallas_call(
        functools.partial(kernel, nb, chunks),
        out_shape=(
            jax.ShapeDtypeStruct((ROW_DEV, nb * span // 2), f32),
            jax.ShapeDtypeStruct((ROW_DEV, cols // 2), f32),
        ),
        in_specs=[pl.BlockSpec(memory_space=pltpu.HBM)] * 2,
        out_specs=(pl.BlockSpec(memory_space=pltpu.VMEM),) * 2,
        scratch_shapes=[
            pltpu.VMEM((toks, span), bf16),
            pltpu.VMEM((cols, span), bf16),
            pltpu.VMEM((4 * toks, quarter), bf16),
            pltpu.VMEM((rows, 4 * toks), bf16),
            pltpu.VMEM((rows, quarter), f32),
            pltpu.VMEM((rows, cols), f32),
            pltpu.VMEM((rows, cols // 2), f32),
            pltpu.VMEM((nb // 2, 2, ROW_DEV, cols // 2), f32),
            pltpu.VMEM((nb // 2, ROW_DEV, cols // 2), f32),
            pltpu.VMEM((nb // 2, ROW_DEV, cols // 2), f32),
            pltpu.VMEM((nb // 2, ROW_DEV, cols // 2), f32),
            pltpu.VMEM((ROW_DEV, cols // 2), f32),
            pltpu.VMEM((ROW_DEV, cols // 2), f32),
            dma((3,)),
            dma((nc, 3)), dma((nc, 3)),
            dma((2, nb)), dma((2, nb)),
            dma((2,)), dma((2,)),
            dma((nc, nb)), dma((nc, nb)),
            dma((nc, nb)), dma((nc, nb)),
            dma((4,)),
            dma((nb // 2,)), dma((nb // 2,)),
            dma((4,)),
        ],
        compiler_params=pltpu.CompilerParams(
            collective_id=0, has_side_effects=True, vmem_limit_bytes=40 * 1024 * 1024
        ),
        cost_estimate=pl.CostEstimate(
            flops=2 * toks * span * cols + 2 * rows * quarter * 4 * toks,
            bytes_accessed=2 * (toks + cols) * span + 2 * ROW_DEV * nb * span,
            transcendentals=0,
        ),
    )(
        pltpu.with_memory_space_constraint(x, pltpu.HBM),
        pltpu.with_memory_space_constraint(w, pltpu.HBM),
    )


def general(x, w, din):
    x_rows = x[:, :ROW_DEV]
    span = x.shape[1]
    b, t, nt = lax.axis_index("blk"), lax.axis_index("tok"), lax.axis_size("tok")
    share, part = din // nt, w.shape[0] // nt
    gram = lax.psum(
        lax.dot_general(
            x_rows, lax.all_gather(x, "blk", axis=1, tiled=True),
            (((0,), (0,)), ((), ())), preferred_element_type=jnp.float32,
        ),
        "tok",
    )
    col_ids = lax.broadcasted_iota(jnp.int32, gram.shape, 1)
    row_ids = lax.broadcasted_iota(jnp.int32, gram.shape, 0)
    reduced = jnp.where(col_ids == b * span + row_ids, gram, OFF_SCALE * gram)
    den = lax.dynamic_slice_in_dim(reduced, t * share, share, 1)
    w_group = lax.dynamic_slice_in_dim(w, t * part, part, 0)
    num = lax.dot_general(
        reduced, lax.all_gather(w_group, "blk", axis=1, tiled=True).astype(jnp.float32),
        (((1,), (1,)), ((), ())), precision=lax.Precision.HIGHEST,
        preferred_element_type=jnp.float32,
    )
    return lax.psum((den, num), "mp")


def solution(mesh):
    nm, nb, nt = mesh.shape["mp"], mesh.shape["blk"], mesh.shape["tok"]

    def local(inputs, down_weight):
        x, w = inputs[0], down_weight[0]
        toks, span = x.shape
        fits = (
            nm == 2 and nt == 2 and nb % 2 == 0 and toks == LANE
            and span % (4 * LANE) == 0 and span >= 8 * LANE
            and w.shape[0] % (4 * LANE) == 0
        )
        if fits:
            return fused(x, w, nb)
        return general(x, w, nb * span)

    return jax.shard_map(
        local,
        mesh=mesh,
        in_specs=(P("mp", "tok", "blk"), P("mp", None, "blk")),
        out_specs=(P("blk", "tok"), P("blk", "tok")),
        check_vma=False,
    )
```

```python
import functools

import jax
import jax.numpy as jnp
from jax import lax
from jax.experimental import pallas as pl
from jax.experimental.pallas import tpu as pltpu
from jax.sharding import PartitionSpec as P

ROW_DEV = 32
OFF_SCALE = 0.9
LANE = 128
MESH = pl.DeviceIdType.MESH


def ds(start, size):
    return pl.ds(pl.multiple_of(start, size), size)


def lanes(start, size):
    return pl.ds(pl.multiple_of(start, LANE), size)


def kernel(
    nb, chunks,
    x_hbm, w_hbm, den, num,
    xv, wv, xq, xwt, g, nloc, n_a, n_s, n_y, n_u, n_c, n_t, n_d,
    ld, xs_send, xs_recv, s1_send, s1_recv, s2_send, s2_recv,
    p_send, p_recv, f_send, f_recv, a_sem, c_send, c_recv, d_sem,
):
    m, b, t = lax.axis_index("mp"), lax.axis_index("blk"), lax.axis_index("tok")
    toks, span = xv.shape
    cols = wv.shape[0]
    quarter = span // 4
    per_half = nb // 2
    s = m * 2 + t
    om, ot = 1 - m, 1 - t
    group = [(om, t), (om, ot), (m, ot)]

    load_x = pltpu.make_async_copy(x_hbm, xv, ld.at[0])
    load_w = pltpu.make_async_copy(w_hbm, wv, ld.at[1])
    load_q = pltpu.make_async_copy(
        x_hbm.at[:, lanes(s * quarter, quarter)], xq.at[ds(s * toks, toks), :], ld.at[2]
    )
    load_x.start()
    load_w.start()
    load_q.start()

    barrier = pltpu.get_barrier_semaphore()
    peers = [(om, b, t), (om, b, ot), (m, b, ot)]
    for k in range(1, nb):
        bp = lax.rem(b + k, nb)
        peers += [(m, bp, t), (m, bp, ot)]
    for peer in peers:
        pl.semaphore_signal(barrier, inc=1, device_id=peer, device_id_type=MESH)
    pl.semaphore_wait(barrier, len(peers))

    def remote(src, dst, send, recv, device):
        return pltpu.make_async_remote_copy(
            src_ref=src, dst_ref=dst, send_sem=send, recv_sem=recv,
            device_id=device, device_id_type=MESH,
        )

    sent = []

    def piece_t(rows, sm, st):
        return xwt.at[rows, lanes((sm * 2 + st) * toks, toks)]

    exchange = []
    for c, (off, width) in enumerate(chunks):
        copies = []
        for k, (pm, pt) in enumerate(group):
            ps = pm * 2 + pt
            copies.append(remote(
                x_hbm.at[:, lanes(ps * quarter + off, width)],
                xq.at[ds(s * toks, toks), off:off + width],
                xs_send.at[c, k], xs_recv.at[c, k], (pm, b, pt),
            ))
        exchange.append(copies)
        sent += copies
    def send_exchange(c):
        for cp in exchange[c]:
            cp.start()

    send_exchange(0)

    load_x.wait()
    mine = ds(b * ROW_DEV, ROW_DEV)
    own_t = jnp.transpose(xv[:, :LANE].astype(jnp.float32))[:ROW_DEV]
    xwt[mine, lanes(s * toks, toks)] = own_t.astype(jnp.bfloat16)
    over_x = remote(
        piece_t(mine, m, t), piece_t(mine, m, t), d_sem.at[2], d_sem.at[3], (om, b, t)
    )
    over_x.start()
    stage1 = []
    for r in range(2):
        copies = []
        for k in range(1, nb):
            bp = lax.rem(b + k, nb)
            piece = piece_t(mine, om if r else m, t)
            cp = remote(piece, piece, s1_send.at[r, k], s1_recv.at[r, k], (m, bp, t))
            copies.append(cp)
        if r:
            over_x.wait_recv()
        for cp in copies:
            cp.start()
        stage1.append(copies)
    send_exchange(1)
    stage2 = []
    for r in range(2):
        for cp in stage1[r]:
            cp.wait_recv()
        piece = piece_t(slice(None), om if r else m, t)
        cp = remote(piece, piece, s2_send.at[r], s2_recv.at[r], (m, b, ot))
        cp.start()
        stage2.append(cp)
    sent += [over_x] + stage1[0] + stage1[1] + stage2

    owner = b // per_half
    base = lax.rem(b, per_half) * span + s * quarter
    place = lax.rem(b, per_half)
    slot = place * 2 + t
    half = cols // 2
    order = [k for r in range(1, per_half) for k in (per_half + r - 1, r)] + [nb - 1, 0]

    def gram_chunk(c):
        off, width = chunks[c]
        for cp in exchange[c]:
            cp.wait_recv()
        if c + 2 < len(chunks):
            send_exchange(c + 2)
        gram = jnp.dot(
            xwt[...], xq[:, off:off + width], preferred_element_type=jnp.float32
        )
        if off == 0:
            row_ids = lax.broadcasted_iota(jnp.int32, gram.shape, 0)
            col_ids = lax.broadcasted_iota(jnp.int32, gram.shape, 1)
            first = jnp.where(s == 0, ROW_DEV, 0)
            on_diag = (col_ids < first) & (row_ids == b * ROW_DEV + col_ids)
            g[:, off:off + width] = jnp.where(on_diag, gram, OFF_SCALE * gram)
        else:
            g[:, off:off + width] = OFF_SCALE * gram
        for k in order:
            side = 1 - owner if k >= per_half else owner
            bp = side * per_half + lax.rem(place + k + 1 if k >= per_half else place + k, per_half)
            src = g.at[ds(bp * ROW_DEV, ROW_DEV), off:off + width]
            dst = den.at[:, lanes(base + off, width)]
            cp = remote(src, dst, p_send.at[c, k], p_recv.at[c, slot], (m, bp, owner))
            if k:
                cp.start()
                sent.append(cp)
            else:
                here = pltpu.make_async_copy(src, dst, p_recv.at[c, slot])
                pl.when(owner == t)(here.start)
                pl.when(owner != t)(cp.start)

    forwards = []

    def forward_chunk(c):
        off, width = chunks[c]
        for j in range(nb):
            i = lax.rem(place + (2 * per_half - j // 2 - 1), per_half)
            core = j % 2
            where = i * 2 + core
            came = den.at[:, lanes(i * span + (m * 2 + core) * quarter + off, width)]
            remote(
                came, came, f_send.at[c, j], p_recv.at[c, where], (om, b, t)
            ).wait_recv()
            cp = remote(came, came, f_send.at[c, j], f_recv.at[c, j], (om, b, t))
            cp.start()
            forwards.append(cp)

    pairs, zb, y = nb // 2, b // 2, lax.rem(b, 2)
    copy_a = remote(
        nloc.at[:, lanes(ot * half, half)], n_a, a_sem.at[0], a_sem.at[1], (m, b, ot)
    )
    copy_y = remote(
        n_s.at[:, 1 - y], n_y, a_sem.at[2], a_sem.at[3], (m, b + 1 - 2 * y, t)
    )
    stage_c = []
    for k in range(1, pairs):
        zp = lax.rem(zb + k, pairs)
        stage_c.append(remote(
            n_u.at[zp], n_c.at[k], c_send.at[k], c_recv.at[k], (m, zp * 2 + y, t)
        ))
    copy_d = remote(n_t, n_d, d_sem.at[0], d_sem.at[1], (om, b, t))

    def product():
        load_w.wait()
        z = lax.dot_general(
            xv[...], wv[...], (((1,), (1,)), ((), ())),
            preferred_element_type=jnp.float32,
        )
        z_hi = z.astype(jnp.bfloat16)
        z_lo = (z - z_hi.astype(jnp.float32)).astype(jnp.bfloat16)
        w_t = jnp.transpose(wv[:, :LANE].astype(jnp.float32))[:ROW_DEV]
        diag = jnp.sum(own_t * own_t, axis=1, keepdims=True)
        rows_t = xwt[:, lanes(s * toks, toks)]
        nloc[...] = OFF_SCALE * (
            jnp.dot(rows_t, z_hi, preferred_element_type=jnp.float32)
            + jnp.dot(rows_t, z_lo, preferred_element_type=jnp.float32)
        )
        nloc[mine, :] = nloc[mine, :] + (1.0 - OFF_SCALE) * diag * w_t
        copy_a.start()

    def over_pair():
        copy_a.wait_recv()
        summed = nloc[:, lanes(t * half, half)] + n_a[...]
        n_s[...] = summed.reshape(n_s.shape)
        copy_y.start()

    def over_blocks():
        copy_y.wait_recv()
        n_u[...] = n_s[:, y] + n_y[...]
        for cp in stage_c:
            cp.start()

    def over_models():
        total = n_u[zb]
        for k, cp in enumerate(stage_c):
            cp.wait_recv()
            total = total + n_c[k + 1]
        n_t[...] = total
        copy_d.start()

    load_q.wait()
    for cp in stage2:
        cp.wait_recv()
    last = len(chunks) - 1
    for c in range(last + 1):
        gram_chunk(c)
        for at, step in enumerate((product, over_pair, over_blocks)):
            if c == min(at, last):
                step()
        if c:
            forward_chunk(c - 1)
    over_models()
    forward_chunk(last)
    sent += [copy_a, copy_y, copy_d] + stage_c

    copy_d.wait_recv()
    num[...] = n_t[...] + n_d[...]
    for cp in forwards:
        cp.wait_recv()
    for cp in sent + forwards:
        cp.wait_send()
    for c, (off, width) in enumerate(chunks):
        src = g.at[mine, off:off + width]
        dst = den.at[:, lanes(base + off, width)]
        cp = remote(src, dst, p_send.at[c, 0], p_recv.at[c, slot], (m, b, ot))
        pl.when(owner != t)(cp.wait_send)


def fused(x, w, nb):
    toks, span = x.shape
    cols = w.shape[0]
    rows = nb * ROW_DEV
    quarter = span // 4
    step = -(-quarter // (4 * LANE)) * LANE
    chunks = [(o, min(step, quarter - o)) for o in range(0, quarter, step)]
    nc = len(chunks)
    dma = pltpu.SemaphoreType.DMA
    f32, bf16 = jnp.float32, jnp.bfloat16
    return pl.pallas_call(
        functools.partial(kernel, nb, chunks),
        out_shape=(
            jax.ShapeDtypeStruct((ROW_DEV, nb * span // 2), f32),
            jax.ShapeDtypeStruct((ROW_DEV, cols // 2), f32),
        ),
        in_specs=[pl.BlockSpec(memory_space=pltpu.HBM)] * 2,
        out_specs=(pl.BlockSpec(memory_space=pltpu.VMEM),) * 2,
        scratch_shapes=[
            pltpu.VMEM((toks, span), bf16),
            pltpu.VMEM((cols, span), bf16),
            pltpu.VMEM((4 * toks, quarter), bf16),
            pltpu.VMEM((rows, 4 * toks), bf16),
            pltpu.VMEM((rows, quarter), f32),
            pltpu.VMEM((rows, cols), f32),
            pltpu.VMEM((rows, cols // 2), f32),
            pltpu.VMEM((nb // 2, 2, ROW_DEV, cols // 2), f32),
            pltpu.VMEM((nb // 2, ROW_DEV, cols // 2), f32),
            pltpu.VMEM((nb // 2, ROW_DEV, cols // 2), f32),
            pltpu.VMEM((nb // 2, ROW_DEV, cols // 2), f32),
            pltpu.VMEM((ROW_DEV, cols // 2), f32),
            pltpu.VMEM((ROW_DEV, cols // 2), f32),
            dma((3,)),
            dma((nc, 3)), dma((nc, 3)),
            dma((2, nb)), dma((2, nb)),
            dma((2,)), dma((2,)),
            dma((nc, nb)), dma((nc, nb)),
            dma((nc, nb)), dma((nc, nb)),
            dma((4,)),
            dma((nb // 2,)), dma((nb // 2,)),
            dma((4,)),
        ],
        compiler_params=pltpu.CompilerParams(
            collective_id=0, has_side_effects=True, vmem_limit_bytes=40 * 1024 * 1024
        ),
        cost_estimate=pl.CostEstimate(
            flops=2 * toks * span * cols + 2 * rows * quarter * 4 * toks,
            bytes_accessed=2 * (toks + cols) * span + 2 * ROW_DEV * nb * span,
            transcendentals=0,
        ),
    )(
        pltpu.with_memory_space_constraint(x, pltpu.HBM),
        pltpu.with_memory_space_constraint(w, pltpu.HBM),
    )


def general(x, w, din):
    x_rows = x[:, :ROW_DEV]
    span = x.shape[1]
    b, t, nt = lax.axis_index("blk"), lax.axis_index("tok"), lax.axis_size("tok")
    share, part = din // nt, w.shape[0] // nt
    gram = lax.psum(
        lax.dot_general(
            x_rows, lax.all_gather(x, "blk", axis=1, tiled=True),
            (((0,), (0,)), ((), ())), preferred_element_type=jnp.float32,
        ),
        "tok",
    )
    col_ids = lax.broadcasted_iota(jnp.int32, gram.shape, 1)
    row_ids = lax.broadcasted_iota(jnp.int32, gram.shape, 0)
    reduced = jnp.where(col_ids == b * span + row_ids, gram, OFF_SCALE * gram)
    den = lax.dynamic_slice_in_dim(reduced, t * share, share, 1)
    w_group = lax.dynamic_slice_in_dim(w, t * part, part, 0)
    num = lax.dot_general(
        reduced, lax.all_gather(w_group, "blk", axis=1, tiled=True).astype(jnp.float32),
        (((1,), (1,)), ((), ())), precision=lax.Precision.HIGHEST,
        preferred_element_type=jnp.float32,
    )
    return lax.psum((den, num), "mp")


def solution(mesh):
    nm, nb, nt = mesh.shape["mp"], mesh.shape["blk"], mesh.shape["tok"]

    def local(inputs, down_weight):
        x, w = inputs[0], down_weight[0]
        toks, span = x.shape
        fits = (
            nm == 2 and nt == 2 and nb % 2 == 0 and toks == LANE
            and span % (4 * LANE) == 0 and span >= 8 * LANE
            and w.shape[0] % (4 * LANE) == 0
        )
        if fits:
            return fused(x, w, nb)
        return general(x, w, nb * span)

    return jax.shard_map(
        local,
        mesh=mesh,
        in_specs=(P("mp", "tok", "blk"), P("mp", None, "blk")),
        out_specs=(P("blk", "tok"), P("blk", "tok")),
        check_vma=False,
    )
```
